256 devices in a mesh: row: 16 (over y, x), col: 8 (over z_hi, core), fiber: 2 (over z_lo).
Axes of the slice: x: 4, y: 4, z: 8 (z_hi: 4, z_lo: 2; z = z_hi * 2 + z_lo), core: 2. Of those that a mesh axis runs over, the one named last changes fastest.
Arguments:
- user_factors: float32 [65536, 128], P(('row', 'col', 'fiber')), may hold values from -3 to 3
- item_factors: bfloat16 [131072, 128], P(('row', 'col')), may hold values from -0.119628906 to 0.119628906
- ratings: bfloat16 [16, 8, 256, 128, 128], P('row', 'col', 'fiber'), may hold values from -2 to 2, as said below
- block_user: int32 [16, 8, 256], P('row', 'col', 'fiber'), may hold values from 0 to 31, as said below
- block_item: int32 [16, 8, 256], P('row', 'col', 'fiber'), may hold values from 0 to 127, as said below
- counts: int32 [65536], P(('row', 'col', 'fiber')), may hold values from 1 to 8192, as said below
Outputs:
- factors: float32 [65536, 128], P(('row', 'col', 'fiber'))
- residual: float32 [65536, 128], P(('row', 'col', 'fiber'))
The draws below stay inside these ranges and needn't reach their ends.
Inputs may be any that keep to these rules, and one draw needn't show every extreme that they name: `block_user`: within one tile (one row index and one column index) the occupied blocks are distinct; each user block index appears in exactly 8 blocks of every tile, which fall on the two fiber halves at random. `block_item`: an item block index within the column slab. counts[u] equals the number of nonzero entries of ratings that belong to user u, over all blocks; some user has every rating of its blocks observed. Every user row of every occupied block has an observed rating; observed ratings have magnitude 0.25 or more.
All inputs are finite; a program needn't handle non-finite values.
Results may differ from the reference program's by a relative error of at most 0.012.
The reference program's roundings to bfloat16 on the way count: a program that leaves them out, or rounds other values in their place, can miss the bound.
Values may be sent and summed in bfloat16 or wider, within the bound.
No kernel may reach another device: no remote copies, remote signals or barrier semaphores. Data moves between devices by JAX's collectives and lax.ppermute only.
A program may use at most 64 MiB of HBM per device.

```python
import jax
import jax.numpy as jnp
from jax import lax

RANK = 128
BLOCK = 128
ITERS = 2
ITEM_DEV = 1024
GRID_ROWS = 16
GRID_COLS = 8
TILE_BLOCKS = 256
USER_BLOCKS = 32
ITEM_BLOCKS = 128
BLOCKS_PER_USER = 8
USERS = 65536
ITEMS = 131072


def layout(key):
    base = jax.random.fold_in(key, 7001)
    tiles = GRID_ROWS * GRID_COLS
    perm_keys = jax.random.split(jax.random.fold_in(base, 1), tiles * USER_BLOCKS)
    perms = jax.vmap(lambda sub: jax.random.permutation(sub, ITEM_BLOCKS))(perm_keys)
    chosen = perms[:, :BLOCKS_PER_USER].reshape(tiles, TILE_BLOCKS).astype(jnp.int32)
    owners = jnp.repeat(jnp.arange(USER_BLOCKS, dtype=jnp.int32), BLOCKS_PER_USER)
    owners = jnp.broadcast_to(owners[None, :], (tiles, TILE_BLOCKS))
    order_keys = jax.random.split(jax.random.fold_in(base, 2), tiles)
    orders = jax.vmap(lambda sub: jax.random.permutation(sub, TILE_BLOCKS))(order_keys)
    users = jnp.take_along_axis(owners, orders, axis=1)
    items = jnp.take_along_axis(chosen, orders, axis=1)
    return (users.reshape(GRID_ROWS, GRID_COLS, TILE_BLOCKS), items.reshape(GRID_ROWS, GRID_COLS, TILE_BLOCKS))


def observed_entries(key):
    users, items = layout(key)
    base = jax.random.fold_in(key, 7002)
    density = jax.random.randint(jax.random.fold_in(base, 1), (USERS,), 1, 9)
    dense_user = jax.random.randint(jax.random.fold_in(base, 4), (), 0, USERS)
    density = jnp.where(jnp.arange(USERS, dtype=jnp.int32) == dense_user, 16, density)
    grid_rows = jnp.arange(GRID_ROWS, dtype=jnp.int32)[:, None, None, None]
    inside = jnp.arange(BLOCK, dtype=jnp.int32)[None, None, None, :]
    user_ids = grid_rows * (USER_BLOCKS * BLOCK) + users[..., None] * BLOCK + inside
    levels = density[user_ids]
    random_bits = jax.random.randint(jax.random.fold_in(base, 2), (GRID_ROWS, GRID_COLS, TILE_BLOCKS, BLOCK, BLOCK), 0, 16)
    forced = jax.random.randint(jax.random.fold_in(base, 3), (GRID_ROWS, GRID_COLS, TILE_BLOCKS, BLOCK), 0, BLOCK)
    column_ids = jnp.arange(BLOCK, dtype=jnp.int32)
    chosen = (random_bits < levels[..., None]) | (column_ids == forced[..., None])
    return (chosen, user_ids)


def draw_block_user(key, part):
    return layout(key)[0]


def draw_block_item(key, part):
    return layout(key)[1]


def draw_counts(key, part):
    chosen, user_ids = observed_entries(key)
    per_row = jnp.sum(chosen.astype(jnp.int32), axis=-1)
    totals = jnp.zeros((USERS,), jnp.int32)
    return totals.at[user_ids.reshape(-1)].add(per_row.reshape(-1))


def draw_ratings(key, part):
    chosen, user_ids = observed_entries(key)
    base = jax.random.fold_in(key, 7003)
    shape = (GRID_ROWS, GRID_COLS, TILE_BLOCKS, BLOCK, BLOCK)
    uniform = jax.random.uniform(jax.random.fold_in(base, 1), shape, jnp.float32)
    coins = jax.random.uniform(jax.random.fold_in(base, 2), shape, jnp.float32)
    signs = jnp.where(coins < 0.5, 1.0, -1.0)
    magnitude = 0.25 + 1.75 * uniform
    values = jnp.where(chosen, signs * magnitude, 0.0)
    return values.astype(jnp.bfloat16)


def block_scale(own_key, shape, cuts, least, top_value):
    factor_of = 1.0
    for position, shards_of in cuts:
        draws = jax.random.uniform(jax.random.fold_in(jax.random.fold_in(own_key, 6), position), (shards_of,), jnp.float32, least / len(cuts), top_value / len(cuts))
        factor_of = factor_of * jnp.repeat(jnp.exp(draws), shape[position] // shards_of).reshape((-1,) + (1,) * (len(shape) - 1 - position))
    return factor_of


def scatter_about(key, dims, spread, bound, shards=(), kind=jnp.bfloat16):
    array = spread * jax.random.normal(key, dims, jnp.float32)
    if shards:
        array = array * block_scale(key, dims, shards, -0.22, 0.18)
    return jnp.clip(array, -bound, bound).astype(kind)


def setup_inputs(seed: int = 0) -> dict:
    key_of = jax.random.split(jax.random.key(seed), 7)
    user_factors = scatter_about(key_of[0], (USERS, RANK), 0.5, 3.0, ((0, 256),), jnp.float32)
    item_factors = scatter_about(key_of[1], (ITEMS, RANK), 0.02, 0.119628906, ((0, 128),))
    ratings = draw_ratings(jax.random.fold_in(key_of[6], 71), 0)
    block_user = draw_block_user(jax.random.fold_in(key_of[6], 71), 0)
    block_item = draw_block_item(jax.random.fold_in(key_of[6], 71), 0)
    counts = draw_counts(jax.random.fold_in(key_of[6], 71), 0)
    return {"user_factors": user_factors, "item_factors": item_factors, "ratings": ratings, "block_user": block_user, "block_item": block_item, "counts": counts}


reg_weight = 4e-4
tiny = 1e-6


def block_terms(slab_values, item_slab, rating_tile, owners, columns, with_ratings):
    block_size = rating_tile.shape[1]
    factor_rank = slab_values.shape[1]
    user_count = slab_values.shape[0] // block_size
    user_rows = slab_values.reshape(user_count, block_size, factor_rank)[owners].astype(jnp.float32)
    item_rows = item_slab.reshape(item_slab.shape[0] // block_size, block_size, factor_rank)[columns].astype(jnp.float32)
    predicted = jnp.einsum("nik,njk->nij", user_rows, item_rows)
    observed = (rating_tile != 0).astype(jnp.float32)
    if with_ratings:
        weights = (rating_tile.astype(jnp.float32) - observed * predicted).astype(jnp.bfloat16)
    else:
        weights = (observed * predicted).astype(jnp.bfloat16)
    weights = lax.optimization_barrier(weights).astype(jnp.float32)
    contribution = jnp.einsum("nij,njk->nik", weights, item_rows)
    summed = jax.ops.segment_sum(contribution, owners, num_segments=user_count)
    return summed.reshape(user_count * block_size, factor_rank)


def apply_all(values, item_factors, ratings, block_user, block_item, with_ratings):
    user_grid = values.reshape(GRID_ROWS, USER_BLOCKS * BLOCK, RANK)
    item_grid = item_factors.reshape(GRID_ROWS, GRID_COLS, ITEM_DEV, RANK)
    col_index = jnp.arange(GRID_COLS, dtype=jnp.int32)

    def per_row(grid_row):
        def per_col(running, grid_col):
            item_slab = item_grid[:, grid_col].reshape(GRID_ROWS * ITEM_DEV, RANK)
            term = block_terms(user_grid[grid_row], item_slab, ratings[grid_row, grid_col], block_user[grid_row, grid_col], block_item[grid_row, grid_col], with_ratings)
            return running + term, None

        initial = jnp.zeros((USER_BLOCKS * BLOCK, RANK), jnp.float32)
        running, unused = lax.scan(per_col, initial, col_index)
        return running

    stacked = lax.map(per_row, jnp.arange(GRID_ROWS, dtype=jnp.int32))
    return stacked.reshape(USERS, RANK)


def reference(user_factors, item_factors, ratings, block_user, block_item, counts):
    damping = reg_weight * counts.astype(jnp.float32)[:, None]
    factors = user_factors
    residual = apply_all(factors.astype(jnp.bfloat16), item_factors, ratings, block_user, block_item, True) - damping * factors
    direction = residual
    squares = jnp.sum(residual * residual, axis=1, keepdims=True)
    for iteration in range(ITERS):
        image = apply_all(direction.astype(jnp.bfloat16), item_factors, ratings, block_user, block_item, False) + damping * direction
        step_size = squares / (jnp.sum(direction * image, axis=1, keepdims=True) + tiny)
        factors = factors + step_size * direction
        residual = residual - step_size * image
        if iteration + 1 < ITERS:
            renewed = jnp.sum(residual * residual, axis=1, keepdims=True)
            direction = residual + (renewed / (squares + tiny)) * direction
            squares = renewed
    return factors, residual
```

```python
import functools

import jax
import jax.numpy as jnp
from jax import lax
from jax.experimental import pallas as pl
from jax.experimental.pallas import tpu as pltpu
from jax.sharding import Mesh, PartitionSpec as P

ITERS = 2
GROUP = 4
AT_ONCE = 4
BLOCKS = 256
LOCAL = 16

FIRST_SCALE = 4.0
LATER_SCALE = 16.0

reg_weight = 0.0004
tiny = 1e-06

RING = ("zh", "zl")
SWAP = [(0, 1), (1, 0)]
VMEM = pl.BlockSpec(memory_space=pltpu.VMEM)
SMEM = pl.BlockSpec(memory_space=pltpu.SMEM)


def swapped(array):
    return lax.ppermute(array, "core", SWAP)


def shifted(array, axis, step):
    return lax.ppermute(array, axis, [(i, (i + step) % 4) for i in range(4)])


def along(near, axis):
    behind = [shifted(piece, axis, 1) for piece in near]
    ahead = [shifted(piece, axis, -1) for piece in near]
    far = [shifted(behind[0], axis, 1), shifted(ahead[1], axis, -1)]
    return [near, ahead, far, behind]


def first_leg(piece, axis):
    behind = shifted(piece, axis, 1)
    ahead = shifted(piece, axis, -1)
    far = shifted(piece, axis, 2)
    return [
        jnp.concatenate([piece, ahead], axis=0),
        jnp.concatenate([far, behind], axis=0),
    ]


def gathered_items(item_factors):
    half = item_factors.shape[0] // 2
    blocks = item_factors.reshape(2, half // 128, 128, 128)
    legs_a = first_leg(blocks[0], "x")
    legs_b = first_leg(blocks[1], "y")
    rows_a = along(legs_a, "y")
    rows_b = along(legs_b, "x")
    own = [piece for row in rows_a + rows_b for piece in row]
    other = [swapped(piece) for piece in own]
    return jnp.concatenate(own + other, axis=0)


def item_places(block_item):
    y, x = lax.axis_index("y"), lax.axis_index("x")
    dy = ((block_item >> 5) - y) & 3
    dx = ((block_item >> 3) - x) & 3
    within = block_item & 3
    place_a = (dy * 4 + dx) * 4 + within
    place_b = 64 + (dx * 4 + dy) * 4 + within
    return jnp.where((block_item >> 2) & 1 == 0, place_a, place_b)


def tables(block_user, block_item):
    own = jnp.stack([block_user, item_places(block_item)])
    other = swapped(own)
    owners = jnp.concatenate([own[0], other[0]])
    places = jnp.concatenate([own[1], other[1] + 128])
    ids = jnp.arange(BLOCKS, dtype=jnp.int32)
    users = jnp.arange(LOCAL, dtype=jnp.int32)
    mine = ((owners >> 2) & 1) == lax.axis_index("core")
    local = jnp.where(mine, ((owners >> 3) << 2) | (owners & 3), LOCAL)
    before = (local[None, :] == local[:, None]) & (ids[None, :] < ids[:, None])
    position = jnp.sum(before.astype(jnp.int32), axis=1)
    members = jnp.sum((local[None, :] == users[:, None]).astype(jnp.int32), axis=1)
    groups = (members + GROUP - 1) // GROUP
    start = jnp.sum(
        jnp.where(users[None, :] < local[:, None], groups[None, :], 0), axis=1
    )
    ends = jnp.sum(
        jnp.where(users[None, :] <= users[:, None], groups[None, :], 0), axis=1
    )
    slot = jnp.where(mine, start * GROUP + position, BLOCKS)
    here = slot[None, :] == ids[:, None]
    slot_block = BLOCKS + jnp.sum(jnp.where(here, ids[None, :] - BLOCKS, 0), axis=1)
    slot_place = jnp.sum(jnp.where(here, places[None, :], 0), axis=1)
    group_ids = jnp.arange(BLOCKS // GROUP, dtype=jnp.int32)
    group_user = jnp.sum((ends[None, :] <= group_ids[:, None]).astype(jnp.int32), axis=1)
    group_user = jnp.minimum(group_user, LOCAL - 1)
    steps = (ends[LOCAL - 1 :] + AT_ONCE - 1) // AT_ONCE
    return slot_block, slot_place, group_user, steps


def terms_kernel(
    with_ratings, slot_block, slot_place, group_user, steps, users, ratings, items, out, total
):
    total[...] = jnp.zeros_like(total)

    def group(number):
        user = group_user[number]
        item_rows, rating_parts = [], []
        for k in range(GROUP):
            block = slot_block[number * GROUP + k]
            item_rows.append(items[slot_place[number * GROUP + k]])
            part = ratings[jnp.minimum(block, BLOCKS - 1)]
            rating_parts.append(jnp.where(block < BLOCKS, part, jnp.bfloat16(0)))
        item_rows = jnp.concatenate(item_rows, axis=0)
        rating = jnp.concatenate(rating_parts, axis=1)
        predicted = lax.dot_general(
            users[user],
            item_rows,
            (((1,), (1,)), ((), ())),
            preferred_element_type=jnp.float32,
        )
        if with_ratings:
            weights = jnp.where(
                rating != 0, rating.astype(jnp.float32) - predicted, 0.0
            ).astype(jnp.bfloat16)
        else:
            weights = jnp.where(rating != 0, predicted.astype(jnp.bfloat16), jnp.bfloat16(0))
        return user, jnp.dot(weights, item_rows, preferred_element_type=jnp.float32)

    def step(number, carry):
        results = [group(number * AT_ONCE + k) for k in range(AT_ONCE)]
        for user, value in results:
            total[user] = total[user] + value
        return carry

    lax.fori_loop(0, steps[0], step, 0)
    if with_ratings:
        out[...] = total[...] * FIRST_SCALE
    else:
        out[...] = total[...] * (LATER_SCALE / largest(users[...]))


def terms(where_to, users, ratings, items, with_ratings):
    return pl.pallas_call(
        functools.partial(terms_kernel, with_ratings),
        out_shape=jax.ShapeDtypeStruct((LOCAL, 128, 128), jnp.float32),
        in_specs=[SMEM, SMEM, SMEM, SMEM, VMEM, VMEM, VMEM],
        out_specs=VMEM,
        scratch_shapes=[pltpu.VMEM((LOCAL, 128, 128), jnp.float32)],
        compiler_params=pltpu.CompilerParams(vmem_limit_bytes=32 << 20),
        cost_estimate=pl.CostEstimate(
            flops=1 << 30, bytes_accessed=18 << 20, transcendentals=0
        ),
        name="terms",
    )(*where_to, users, ratings, items)


def largest(direction):
    size = jnp.max(jnp.abs(direction.astype(jnp.float32)), axis=-1, keepdims=True)
    return jnp.maximum(size, 1e-30)


def to_all(direction, out, unit_out):
    rounded = direction.astype(jnp.bfloat16)
    unit_out[...] = largest(rounded) / LATER_SCALE
    for k in range(out.shape[0]):
        out[k] = rounded


def first_kernel(summed, counts, factors, sent, unit_out, residual_out, squares_out):
    damping = reg_weight * counts[...].astype(jnp.float32)
    residual = summed[...] / FIRST_SCALE - damping * factors[...]
    residual_out[...] = residual
    squares_out[...] = jnp.sum(residual * residual, axis=1, keepdims=True)
    to_all(residual, sent, unit_out)


def stepped(summed, unit, counts, factors, residual, direction, squares):
    damping = reg_weight * counts[...].astype(jnp.float32)
    image = summed[...] * unit[...] + damping * direction
    step_size = squares / (jnp.sum(direction * image, axis=1, keepdims=True) + tiny)
    return factors + step_size * direction, residual - step_size * image


def middle_kernel(
    summed, unit, counts, factors, residual, direction, squares,
    sent, unit_out, factors_out, residual_out, direction_out, squares_out,
):
    new_factors, new_residual = stepped(
        summed, unit, counts, factors[...], residual[...], direction[...], squares[...]
    )
    renewed = jnp.sum(new_residual * new_residual, axis=1, keepdims=True)
    new_direction = new_residual + renewed / (squares[...] + tiny) * direction[...]
    factors_out[...] = new_factors
    residual_out[...] = new_residual
    direction_out[...] = new_direction
    squares_out[...] = renewed
    to_all(new_direction, sent, unit_out)


def last_kernel(
    summed, unit, counts, factors, residual, direction, squares, factors_out, residual_out
):
    new_factors, new_residual = stepped(
        summed, unit, counts, factors[...], residual[...], direction[...], squares[...]
    )
    factors_out[...] = new_factors
    residual_out[...] = new_residual


def update(kernel, outs, *args):
    return pl.pallas_call(
        kernel,
        out_shape=outs,
        in_specs=[VMEM] * len(args),
        out_specs=[VMEM] * len(outs),
        compiler_params=pltpu.CompilerParams(vmem_limit_bytes=16 << 20),
        name=kernel.__name__,
    )(*args)


def exchanged(pieces):
    return lax.all_to_all(pieces, RING, 0, 0, tiled=True)


def per_device(user_factors, item_factors, ratings, block_user, block_item, counts):
    own_users, rank = user_factors.shape
    chips = lax.axis_size(RING)
    vector = jax.ShapeDtypeStruct((own_users, rank), jnp.float32)
    scalar = jax.ShapeDtypeStruct((own_users, 1), jnp.float32)
    pieces = jax.ShapeDtypeStruct((chips, own_users, rank), jnp.bfloat16)

    own_ratings = ratings[0, 0]
    all_ratings = jnp.concatenate([own_ratings, swapped(own_ratings)], axis=0)
    where_to = tables(block_user[0, 0], block_item[0, 0])
    items = gathered_items(item_factors)
    counts = counts[:, None]

    def sums(sent, with_ratings):
        users = exchanged(sent).reshape(LOCAL, 128, rank)
        value = terms(where_to, users, all_ratings, items, with_ratings)
        parts = exchanged(value.reshape(chips, own_users, rank).astype(jnp.float16))
        return jnp.sum(parts.astype(jnp.float32), axis=0)

    start = user_factors.astype(jnp.bfloat16)
    summed = sums(jnp.broadcast_to(start[None], pieces.shape), True)
    sent, unit, residual, squares = update(
        first_kernel, [pieces, scalar, vector, scalar], summed, counts, user_factors
    )
    factors, direction = user_factors, residual
    for iteration in range(ITERS):
        summed = sums(sent, False)
        state = (summed, unit, counts, factors, residual, direction, squares)
        if iteration + 1 < ITERS:
            sent, unit, factors, residual, direction, squares = update(
                middle_kernel, [pieces, scalar, vector, vector, vector, scalar], *state
            )
        else:
            factors, residual = update(last_kernel, [vector, vector], *state)
    return factors, residual


def solution(mesh):
    fine = Mesh(
        mesh.devices.reshape(4, 4, 4, 2, 2), ("y", "x", "zh", "core", "zl")
    )
    row, col = ("y", "x"), ("zh", "core")
    every = row + col + ("zl",)
    return jax.shard_map(
        per_device,
        mesh=fine,
        in_specs=(
            P(every, None),
            P(row + col, None),
            P(row, col, "zl", None, None),
            P(row, col, "zl"),
            P(row, col, "zl"),
            P(every),
        ),
        out_specs=(P(every, None), P(every, None)),
        check_vma=False,
    )
```

```python
import functools

import jax
import jax.numpy as jnp
from jax import lax
from jax.experimental import pallas as pl
from jax.experimental.pallas import tpu as pltpu
from jax.sharding import Mesh, PartitionSpec as P

ITERS = 2
GROUP = 4
AT_ONCE = 4
BLOCKS = 256
STEP_BLOCKS = GROUP * AT_ONCE
ROOMS = 3
STEPS = BLOCKS // STEP_BLOCKS
LOCAL = 16

FIRST_SCALE = 4.0
LATER_SCALE = 16.0

reg_weight = 0.0004
tiny = 1e-06

RING = ("zh", "zl")
SWAP = [(0, 1), (1, 0)]
VMEM = pl.BlockSpec(memory_space=pltpu.VMEM)
ANY = pl.BlockSpec(memory_space=pl.ANY)
SMEM = pl.BlockSpec(memory_space=pltpu.SMEM)


def in_hbm(array):
    return pltpu.with_memory_space_constraint(array, pltpu.HBM)


def swapped(array):
    return lax.ppermute(array, "core", SWAP)


def turned(array, leg, step):
    pairs = []
    for y in range(4):
        for x in range(4):
            for core in range(2):
                along_x = core == leg
                to_y = y if along_x else (y + step) % 4
                to_x = (x + step) % 4 if along_x else x
                pairs.append(((y * 4 + x) * 2 + core, (to_y * 4 + to_x) * 2 + core))
    return lax.ppermute(array, ("y", "x", "core"), pairs)


def around(near, leg):
    half = near.shape[0] // 2
    behind = turned(near, leg, 1)
    ahead = turned(near, leg, -1)
    far = [turned(behind[:half], leg, 1), turned(ahead[half:], leg, -1)]
    return [near, ahead, *far, behind]


def gathered_items(item_factors, get_start, get_ratings):
    blocks = item_factors.reshape(item_factors.shape[0] // 128, 128, 128)
    line = jnp.concatenate(around(blocks, 0), axis=0)
    half = line.shape[0] // 2
    behind, ahead = turned(line, 1, 1), turned(line, 1, -1)
    users = get_start(line)
    ratings = get_ratings()
    behind, ahead, ratings = lax.optimization_barrier((behind, ahead, ratings))
    far = [turned(behind[:half], 1, 1), turned(ahead[half:], 1, -1)]
    *far, users = lax.optimization_barrier((*far, users))
    own = [line, ahead, *far, behind]
    other = [swapped(piece) for piece in own]
    return own + other, users, ratings


def item_places(block_item):
    y, x, core = lax.axis_index("y"), lax.axis_index("x"), lax.axis_index("core")
    dy = ((block_item >> 5) - y) & 3
    dx = ((block_item >> 3) - x) & 3
    first, second = jnp.where(core == 0, dx, dy), jnp.where(core == 0, dy, dx)
    return (second * 4 + first) * 8 + (block_item & 7)


def tables(block_user, block_item):
    own = jnp.stack([block_user, item_places(block_item)])
    other = swapped(own)
    owners = jnp.concatenate([own[0], other[0]])
    places = jnp.concatenate([own[1], other[1] + 128])
    ids = jnp.arange(BLOCKS, dtype=jnp.int32)
    users = jnp.arange(LOCAL, dtype=jnp.int32)
    mine = ((owners >> 2) & 1) == lax.axis_index("core")
    local = jnp.where(mine, ((owners >> 3) << 2) | (owners & 3), LOCAL)
    before = (local[None, :] == local[:, None]) & (ids[None, :] < ids[:, None])
    position = jnp.sum(before.astype(jnp.int32), axis=1)
    members = jnp.sum((local[None, :] == users[:, None]).astype(jnp.int32), axis=1)
    groups = (members + GROUP - 1) // GROUP
    start = jnp.sum(
        jnp.where(users[None, :] < local[:, None], groups[None, :], 0), axis=1
    )
    ends = jnp.sum(
        jnp.where(users[None, :] <= users[:, None], groups[None, :], 0), axis=1
    )
    slot = jnp.where(mine, start * GROUP + position, BLOCKS)
    here = mine[None, :] & (slot[None, :] == ids[:, None])
    slot_block = BLOCKS + jnp.sum(jnp.where(here, ids[None, :] - BLOCKS, 0), axis=1)
    slot_place = jnp.sum(jnp.where(here, places[None, :], 0), axis=1)
    group_ids = jnp.arange(BLOCKS // GROUP, dtype=jnp.int32)
    group_user = jnp.sum((ends[None, :] <= group_ids[:, None]).astype(jnp.int32), axis=1)
    group_user = jnp.minimum(group_user, LOCAL - 1)
    steps = (ends[LOCAL - 1 :] + AT_ONCE - 1) // AT_ONCE
    return slot_block, slot_place, group_user, steps


OUT = jax.ShapeDtypeStruct((LOCAL, 128, 128), jnp.float32)
TOTAL = pltpu.VMEM((LOCAL, 128, 128), jnp.float32)
RATING_ROOMS = pltpu.VMEM((ROOMS, AT_ONCE, 128, GROUP * 128), jnp.bfloat16)
ITEM_ROOMS = pltpu.VMEM((ROOMS, AT_ONCE, GROUP * 128, 128), jnp.bfloat16)
ROOM_SEMS = pltpu.SemaphoreType.DMA((ROOMS,))
PARAMS = pltpu.CompilerParams(vmem_limit_bytes=24 << 20)
COST = pl.CostEstimate(flops=1 << 30, bytes_accessed=12 << 20, transcendentals=0)


def sort_kernel(slot_block, steps, own, other, *refs):
    out, whole, rooms, sems, out_sems = refs[-5:]
    count = steps[0]
    half = BLOCKS // 2
    copies = [
        pltpu.make_async_copy(own, whole.at[pl.ds(0, half)], sems.at[0]),
        pltpu.make_async_copy(other, whole.at[pl.ds(half, half)], sems.at[1]),
    ]

    @pl.when(count > 0)
    def _():
        for copy in copies:
            copy.start()
        for copy in copies:
            copy.wait()

    def outgoing(number):
        room = lax.rem(number, ROOMS)
        return pltpu.make_async_copy(rooms.at[room], out.at[number], out_sems.at[room])

    def step(number, carry):
        room = lax.rem(number, ROOMS)

        @pl.when(number >= ROOMS)
        def _():
            outgoing(number - ROOMS).wait()

        for k in range(STEP_BLOCKS):
            block = slot_block[number * STEP_BLOCKS + k]
            values = whole[jnp.minimum(block, BLOCKS - 1)]
            lane = (k % GROUP) * 128
            rooms[room, k // GROUP, :, lane : lane + 128] = jnp.where(
                block < BLOCKS, values, jnp.bfloat16(0)
            )
        outgoing(number).start()
        return carry

    lax.fori_loop(0, count, step, 0)
    for back in range(1, ROOMS + 1):

        @pl.when(count >= back)
        def _():
            outgoing(jnp.maximum(count - back, 0)).wait()


def in_order(slot_block, steps, own, other, *earlier):
    return pl.pallas_call(
        sort_kernel,
        out_shape=pltpu.HBM((STEPS, AT_ONCE, 128, GROUP * 128), jnp.bfloat16),
        in_specs=[SMEM] * 2 + [ANY] * (2 + len(earlier)),
        out_specs=ANY,
        input_output_aliases={4: 0} if earlier else {},
        scratch_shapes=[
            pltpu.VMEM((BLOCKS, 128, 128), jnp.bfloat16),
            RATING_ROOMS,
            pltpu.SemaphoreType.DMA((2,)),
            ROOM_SEMS,
        ],
        compiler_params=PARAMS,
        cost_estimate=pl.CostEstimate(flops=0, bytes_accessed=20 << 20, transcendentals=0),
        name="in_order",
    )(slot_block, steps, in_hbm(own), in_hbm(other), *[in_hbm(array) for array in earlier])


def product(with_ratings, user_rows, rating, item_rows):
    predicted = lax.dot_general(
        user_rows, item_rows, (((1,), (1,)), ((), ())), preferred_element_type=jnp.float32
    )
    if with_ratings:
        weights = jnp.where(
            rating != 0, rating.astype(jnp.float32) - predicted, 0.0
        ).astype(jnp.bfloat16)
    else:
        weights = jnp.where(rating != 0, predicted.astype(jnp.bfloat16), jnp.bfloat16(0))
    return jnp.dot(weights, item_rows, preferred_element_type=jnp.float32)


def incoming(source, rooms, sems, number):
    room = lax.rem(number, ROOMS)
    return pltpu.make_async_copy(
        source.at[jnp.minimum(number, STEPS - 1)], rooms.at[room], sems.at[room]
    )


def first_terms_kernel(slot_place, group_user, steps, users, ratings, *refs):
    *pieces, out, sorted_items, total, whole, rating_rooms, item_rooms, sems, in_sems, out_sems = refs
    count = steps[0]
    copies, place = [], 0
    for number, piece in enumerate(pieces):
        extent = piece.shape[0]
        copies.append(
            pltpu.make_async_copy(piece, whole.at[pl.ds(place, extent)], sems.at[number])
        )
        place += extent
    for copy in copies:
        copy.start()
    for ahead in range(ROOMS - 1):
        incoming(ratings, rating_rooms, in_sems, ahead).start()
    total[...] = jnp.zeros_like(total)
    for copy in copies:
        copy.wait()

    def outgoing(number):
        room = lax.rem(number, ROOMS)
        return pltpu.make_async_copy(
            item_rooms.at[room], sorted_items.at[number], out_sems.at[room]
        )

    def step(number, carry):
        room = lax.rem(number, ROOMS)

        @pl.when(number >= ROOMS)
        def _():
            outgoing(number - ROOMS).wait()

        incoming(ratings, rating_rooms, in_sems, number + ROOMS - 1).start()
        incoming(ratings, rating_rooms, in_sems, number).wait()
        results = []
        for k in range(AT_ONCE):
            first = (number * AT_ONCE + k) * GROUP
            item_rows = jnp.concatenate(
                [whole[slot_place[first + i]] for i in range(GROUP)], axis=0
            )
            item_rooms[room, k] = item_rows
            user = group_user[number * AT_ONCE + k]
            start = users[user].astype(jnp.bfloat16)
            results.append((user, product(True, start, rating_rooms[room, k], item_rows)))
        for user, value in results:
            total[user] = total[user] + value
        outgoing(number).start()
        return carry

    lax.fori_loop(0, count, step, 0)
    for ahead in range(ROOMS - 1):
        incoming(ratings, rating_rooms, in_sems, count + ahead).wait()
    out[...] = total[...] * FIRST_SCALE
    for back in range(1, ROOMS + 1):

        @pl.when(count >= back)
        def _():
            outgoing(jnp.maximum(count - back, 0)).wait()


def later_terms_kernel(
    group_user, steps, users, ratings, sorted_items,
    out, total, rating_rooms, item_rooms, in_sems, item_sems,
):
    count = steps[0]

    def fetches(number):
        return (
            incoming(ratings, rating_rooms, in_sems, number),
            incoming(sorted_items, item_rooms, item_sems, number),
        )

    for ahead in range(ROOMS - 1):
        for copy in fetches(ahead):
            copy.start()
    total[...] = jnp.zeros_like(total)

    def step(number, carry):
        room = lax.rem(number, ROOMS)
        for copy in fetches(number + ROOMS - 1):
            copy.start()
        for copy in fetches(number):
            copy.wait()
        results = []
        for k in range(AT_ONCE):
            user = group_user[number * AT_ONCE + k]
            value = product(False, users[user], rating_rooms[room, k], item_rooms[room, k])
            results.append((user, value))
        for user, value in results:
            total[user] = total[user] + value
        return carry

    lax.fori_loop(0, count, step, 0)
    for ahead in range(ROOMS - 1):
        for copy in fetches(count + ahead):
            copy.wait()
    out[...] = total[...] * (LATER_SCALE / largest(users[...]))


def first_terms(where_to, users, ratings, pieces):
    return pl.pallas_call(
        first_terms_kernel,
        out_shape=[OUT, pltpu.HBM((STEPS, AT_ONCE, GROUP * 128, 128), jnp.bfloat16)],
        in_specs=[SMEM] * 3 + [VMEM] + [ANY] * (1 + len(pieces)),
        out_specs=[VMEM, ANY],
        scratch_shapes=[
            TOTAL,
            pltpu.VMEM((BLOCKS, 128, 128), jnp.bfloat16),
            RATING_ROOMS,
            ITEM_ROOMS,
            pltpu.SemaphoreType.DMA((len(pieces),)),
            ROOM_SEMS,
            ROOM_SEMS,
        ],
        compiler_params=PARAMS,
        cost_estimate=COST,
        name="first_terms",
    )(*where_to, users, in_hbm(ratings), *pieces)


def later_terms(where_to, users, ratings, items):
    return pl.pallas_call(
        later_terms_kernel,
        out_shape=OUT,
        in_specs=[SMEM] * 2 + [VMEM] + [ANY] * 2,
        out_specs=VMEM,
        scratch_shapes=[TOTAL, RATING_ROOMS, ITEM_ROOMS, ROOM_SEMS, ROOM_SEMS],
        compiler_params=PARAMS,
        cost_estimate=COST,
        name="later_terms",
    )(*where_to, users, in_hbm(ratings), in_hbm(items))


def largest(direction):
    size = jnp.max(jnp.abs(direction.astype(jnp.float32)), axis=-1, keepdims=True)
    return jnp.maximum(size, 1e-30)


def to_all(direction, out, unit_out):
    rounded = direction.astype(jnp.bfloat16)
    unit_out[...] = largest(rounded) / LATER_SCALE
    for k in range(out.shape[0]):
        out[k] = rounded


def first_kernel(summed, counts, factors, sent, unit_out, residual_out, squares_out):
    damping = reg_weight * counts[...].astype(jnp.float32)
    residual = summed[...] / FIRST_SCALE - damping * factors[...]
    residual_out[...] = residual
    squares_out[...] = jnp.sum(residual * residual, axis=1, keepdims=True)
    to_all(residual, sent, unit_out)


def stepped(summed, unit, counts, factors, residual, direction, squares):
    damping = reg_weight * counts[...].astype(jnp.float32)
    image = summed[...] * unit[...] + damping * direction
    step_size = squares / (jnp.sum(direction * image, axis=1, keepdims=True) + tiny)
    return factors + step_size * direction, residual - step_size * image


def middle_kernel(
    summed, unit, counts, factors, residual, direction, squares,
    sent, unit_out, factors_out, residual_out, direction_out, squares_out,
):
    new_factors, new_residual = stepped(
        summed, unit, counts, factors[...], residual[...], direction[...], squares[...]
    )
    renewed = jnp.sum(new_residual * new_residual, axis=1, keepdims=True)
    new_direction = new_residual + renewed / (squares[...] + tiny) * direction[...]
    factors_out[...] = new_factors
    residual_out[...] = new_residual
    direction_out[...] = new_direction
    squares_out[...] = renewed
    to_all(new_direction, sent, unit_out)


def last_kernel(
    summed, unit, counts, factors, residual, direction, squares, factors_out, residual_out
):
    new_factors, new_residual = stepped(
        summed, unit, counts, factors[...], residual[...], direction[...], squares[...]
    )
    factors_out[...] = new_factors
    residual_out[...] = new_residual


def update(kernel, outs, *args):
    return pl.pallas_call(
        kernel,
        out_shape=outs,
        in_specs=[VMEM] * len(args),
        out_specs=[VMEM] * len(outs),
        compiler_params=pltpu.CompilerParams(vmem_limit_bytes=16 << 20),
        name=kernel.__name__,
    )(*args)


def exchanged(pieces):
    return lax.all_to_all(pieces, RING, 0, 0, tiled=True)


def per_device(user_factors, item_factors, ratings, block_user, block_item, counts):
    own_users, rank = user_factors.shape
    chips = lax.axis_size(RING)
    vector = jax.ShapeDtypeStruct((own_users, rank), jnp.float32)
    scalar = jax.ShapeDtypeStruct((own_users, 1), jnp.float32)
    copies = jax.ShapeDtypeStruct((chips, own_users, rank), jnp.bfloat16)

    own_ratings = ratings[0, 0]
    slot_block, slot_place, group_user, steps = tables(block_user[0, 0], block_item[0, 0])
    counts = counts[:, None]

    def received(sent):
        return exchanged(sent).reshape(LOCAL, 128, rank)

    def summed_up(value):
        parts = exchanged(value.reshape(chips, own_users, rank).astype(jnp.float16))
        return jnp.sum(parts.astype(jnp.float32), axis=0)

    def get_start(line):
        start, unused = lax.optimization_barrier((user_factors, line))
        start = start.astype(jnp.bfloat16)
        return received(jnp.broadcast_to(start[None], copies.shape))

    other_ratings = swapped(own_ratings)
    early = steps * lax.axis_index("core")

    def get_ratings():
        return in_order(slot_block, early, own_ratings, other_ratings)

    pieces, users, all_ratings = gathered_items(item_factors, get_start, get_ratings)
    all_ratings = in_order(
        slot_block, steps - early, own_ratings, other_ratings, all_ratings
    )
    value, items = first_terms(
        (slot_place, group_user, steps), users, all_ratings, pieces
    )
    sent, unit, residual, squares = update(
        first_kernel,
        [copies, scalar, vector, scalar],
        summed_up(value),
        counts,
        user_factors,
    )
    factors, direction = user_factors, residual
    for iteration in range(ITERS):
        summed = summed_up(
            later_terms((group_user, steps), received(sent), all_ratings, items)
        )
        state = (summed, unit, counts, factors, residual, direction, squares)
        if iteration + 1 < ITERS:
            sent, unit, factors, residual, direction, squares = update(
                middle_kernel, [copies, scalar, vector, vector, vector, scalar], *state
            )
        else:
            factors, residual = update(last_kernel, [vector, vector], *state)
    return factors, residual


def solution(mesh):
    fine = Mesh(
        mesh.devices.reshape(4, 4, 4, 2, 2), ("y", "x", "zh", "core", "zl")
    )
    row, col = ("y", "x"), ("zh", "core")
    every = row + col + ("zl",)
    return jax.shard_map(
        per_device,
        mesh=fine,
        in_specs=(
            P(every, None),
            P(row + col, None),
            P(row, col, "zl", None, None),
            P(row, col, "zl"),
            P(row, col, "zl"),
            P(every),
        ),
        out_specs=(P(every, None), P(every, None)),
        check_vma=False,
    )
```

```python
import functools

import jax
import jax.numpy as jnp
from jax import lax
from jax.experimental import pallas as pl
from jax.experimental.pallas import tpu as pltpu
from jax.sharding import Mesh, PartitionSpec as P

ITERS = 2
GROUP = 8
AT_ONCE = 4
BLOCKS = 256
STEP_BLOCKS = GROUP * AT_ONCE
ROOMS = 3
STEPS = BLOCKS // STEP_BLOCKS
LOCAL = 16

FIRST_SCALE = 4.0
LATER_SCALE = 16.0

reg_weight = 0.0004
tiny = 1e-06

RING = ("zh", "zl")
SWAP = [(0, 1), (1, 0)]
VMEM = pl.BlockSpec(memory_space=pltpu.VMEM)
ANY = pl.BlockSpec(memory_space=pl.ANY)
SMEM = pl.BlockSpec(memory_space=pltpu.SMEM)


def in_hbm(array):
    return pltpu.with_memory_space_constraint(array, pltpu.HBM)


def swapped(array):
    return lax.ppermute(array, "core", SWAP)


def turned(array, leg, step):
    pairs = []
    for y in range(4):
        for x in range(4):
            for core in range(2):
                along_x = core == leg
                to_y = y if along_x else (y + step) % 4
                to_x = (x + step) % 4 if along_x else x
                pairs.append(((y * 4 + x) * 2 + core, (to_y * 4 + to_x) * 2 + core))
    return lax.ppermute(array, ("y", "x", "core"), pairs)


def around(near, leg):
    half = near.shape[0] // 2
    behind = turned(near, leg, 1)
    ahead = turned(near, leg, -1)
    far = [turned(behind[:half], leg, 1), turned(ahead[half:], leg, -1)]
    return [near, ahead, *far, behind]


def gathered_items(item_factors, damping, get_start, get_ratings):
    blocks = item_factors.reshape(item_factors.shape[0] // 128, 128, 128)
    line = jnp.concatenate(around(blocks, 0), axis=0)
    half = line.shape[0] // 2
    behind, ahead = turned(line, 1, 1), turned(line, 1, -1)
    users = get_start(line)
    ratings = get_ratings()
    far = [turned(behind[:half], 1, 1), turned(ahead[half:], 1, -1)]
    *far, users, ratings, damping = lax.optimization_barrier((*far, users, ratings, damping))
    own = [line, ahead, *far, behind]
    other = [swapped(piece) for piece in own]
    return own + other, users, ratings, damping


def item_places(block_item):
    y, x, core = lax.axis_index("y"), lax.axis_index("x"), lax.axis_index("core")
    dy = ((block_item >> 5) - y) & 3
    dx = ((block_item >> 3) - x) & 3
    first, second = jnp.where(core == 0, dx, dy), jnp.where(core == 0, dy, dx)
    return (second * 4 + first) * 8 + (block_item & 7)


def tables(block_user, block_item):
    own = jnp.stack([block_user, item_places(block_item)])
    other = swapped(own)
    owners = jnp.concatenate([own[0], other[0]])
    places = jnp.concatenate([own[1], other[1] + 128])
    ids = jnp.arange(BLOCKS, dtype=jnp.int32)
    users = jnp.arange(LOCAL, dtype=jnp.int32)
    mine = ((owners >> 2) & 1) == lax.axis_index("core")
    local = jnp.where(mine, ((owners >> 3) << 2) | (owners & 3), LOCAL)
    before = (local[None, :] == local[:, None]) & (ids[None, :] < ids[:, None])
    position = jnp.sum(before.astype(jnp.int32), axis=1)
    members = jnp.sum((local[None, :] == users[:, None]).astype(jnp.int32), axis=1)
    groups = (members + GROUP - 1) // GROUP
    start = jnp.sum(
        jnp.where(users[None, :] < local[:, None], groups[None, :], 0), axis=1
    )
    ends = jnp.sum(
        jnp.where(users[None, :] <= users[:, None], groups[None, :], 0), axis=1
    )
    slot = jnp.where(mine, start * GROUP + position, BLOCKS)
    here = mine[None, :] & (slot[None, :] == ids[:, None])
    slot_block = BLOCKS + jnp.sum(jnp.where(here, ids[None, :] - BLOCKS, 0), axis=1)
    slot_place = jnp.sum(jnp.where(here, places[None, :], 0), axis=1)
    group_ids = jnp.arange(BLOCKS // GROUP, dtype=jnp.int32)
    group_user = jnp.sum((ends[None, :] <= group_ids[:, None]).astype(jnp.int32), axis=1)
    group_user = jnp.minimum(group_user, LOCAL - 1)
    steps = (ends[LOCAL - 1 :] + AT_ONCE - 1) // AT_ONCE
    return slot_block, slot_place, group_user, steps


OUT = jax.ShapeDtypeStruct((LOCAL, 128, 128), jnp.float32)
TOTAL = pltpu.VMEM((LOCAL, 128, 128), jnp.float32)
RATING_ROOMS = pltpu.VMEM((ROOMS, AT_ONCE, 128, GROUP * 128), jnp.bfloat16)
ITEM_ROOMS = pltpu.VMEM((ROOMS, AT_ONCE, GROUP * 128, 128), jnp.bfloat16)
ROOM_SEMS = pltpu.SemaphoreType.DMA((ROOMS,))
PARAMS = pltpu.CompilerParams(vmem_limit_bytes=24 << 20)
COST = pl.CostEstimate(flops=1 << 30, bytes_accessed=12 << 20, transcendentals=0)


def sort_kernel(slot_block, steps, own, other, *refs):
    out, whole, rooms, sems, out_sems = refs[-5:]
    count = steps[0]
    half = BLOCKS // 2
    copies = [
        pltpu.make_async_copy(own, whole.at[pl.ds(0, half)], sems.at[0]),
        pltpu.make_async_copy(other, whole.at[pl.ds(half, half)], sems.at[1]),
    ]

    @pl.when(count > 0)
    def _():
        for copy in copies:
            copy.start()
        for copy in copies:
            copy.wait()

    def outgoing(number):
        room = lax.rem(number, ROOMS)
        return pltpu.make_async_copy(rooms.at[room], out.at[number], out_sems.at[room])

    def step(number, carry):
        room = lax.rem(number, ROOMS)

        @pl.when(number >= ROOMS)
        def _():
            outgoing(number - ROOMS).wait()

        for k in range(STEP_BLOCKS):
            block = slot_block[number * STEP_BLOCKS + k]
            values = whole[jnp.minimum(block, BLOCKS - 1)]
            lane = (k % GROUP) * 128
            rooms[room, k // GROUP, :, lane : lane + 128] = jnp.where(
                block < BLOCKS, values, jnp.bfloat16(0)
            )
        outgoing(number).start()
        return carry

    lax.fori_loop(0, count, step, 0)
    for back in range(1, ROOMS + 1):

        @pl.when(count >= back)
        def _():
            outgoing(jnp.maximum(count - back, 0)).wait()


def in_order(slot_block, steps, own, other, *earlier):
    return pl.pallas_call(
        sort_kernel,
        out_shape=pltpu.HBM((STEPS, AT_ONCE, 128, GROUP * 128), jnp.bfloat16),
        in_specs=[SMEM] * 2 + [ANY] * (2 + len(earlier)),
        out_specs=ANY,
        input_output_aliases={4: 0} if earlier else {},
        scratch_shapes=[
            pltpu.VMEM((BLOCKS, 128, 128), jnp.bfloat16),
            RATING_ROOMS,
            pltpu.SemaphoreType.DMA((2,)),
            ROOM_SEMS,
        ],
        compiler_params=PARAMS,
        cost_estimate=pl.CostEstimate(flops=0, bytes_accessed=20 << 20, transcendentals=0),
        name="in_order",
    )(slot_block, steps, in_hbm(own), in_hbm(other), *[in_hbm(array) for array in earlier])


def product(with_ratings, user_rows, rating, item_rows):
    predicted = lax.dot_general(
        user_rows, item_rows, (((1,), (1,)), ((), ())), preferred_element_type=jnp.float32
    )
    if with_ratings:
        weights = jnp.where(
            rating != 0, rating.astype(jnp.float32) - predicted, 0.0
        ).astype(jnp.bfloat16)
    else:
        weights = jnp.where(rating != 0, predicted.astype(jnp.bfloat16), jnp.bfloat16(0))
    return jnp.dot(weights, item_rows, preferred_element_type=jnp.float32)


def incoming(source, rooms, sems, number):
    room = lax.rem(number, ROOMS)
    return pltpu.make_async_copy(
        source.at[jnp.minimum(number, STEPS - 1)], rooms.at[room], sems.at[room]
    )


def first_terms_kernel(slot_place, group_user, steps, users, ratings, *refs):
    *pieces, out, sorted_items, total, whole, rating_rooms, item_rooms, sems, in_sems, out_sems = refs
    count = steps[0]
    copies, place = [], 0
    for number, piece in enumerate(pieces):
        extent = piece.shape[0]
        copies.append(
            pltpu.make_async_copy(piece, whole.at[pl.ds(place, extent)], sems.at[number])
        )
        place += extent
    for copy in copies:
        copy.start()
    def fetch(number):
        @pl.when(number < count)
        def _():
            incoming(ratings, rating_rooms, in_sems, number).start()

    for ahead in range(ROOMS - 1):
        fetch(ahead)
    total[...] = jnp.zeros_like(total)
    for copy in copies:
        copy.wait()

    def outgoing(number):
        room = lax.rem(number, ROOMS)
        return pltpu.make_async_copy(
            item_rooms.at[room], sorted_items.at[number], out_sems.at[room]
        )

    def step(number, carry):
        room = lax.rem(number, ROOMS)

        @pl.when(number >= ROOMS)
        def _():
            outgoing(number - ROOMS).wait()

        fetch(number + ROOMS - 1)
        incoming(ratings, rating_rooms, in_sems, number).wait()
        results = []
        for k in range(AT_ONCE):
            first = (number * AT_ONCE + k) * GROUP
            item_rows = jnp.concatenate(
                [whole[slot_place[first + i]] for i in range(GROUP)], axis=0
            )
            item_rooms[room, k] = item_rows
            user = group_user[number * AT_ONCE + k]
            start = users[user].astype(jnp.bfloat16)
            results.append((user, product(True, start, rating_rooms[room, k], item_rows)))
        for user, value in results:
            total[user] = total[user] + value
        outgoing(number).start()
        return carry

    lax.fori_loop(0, count, step, 0)
    out[...] = total[...] * FIRST_SCALE
    for back in range(1, ROOMS + 1):

        @pl.when(count >= back)
        def _():
            outgoing(jnp.maximum(count - back, 0)).wait()


def later_terms_kernel(
    group_user, steps, users, ratings, sorted_items,
    out, total, rating_rooms, item_rooms, in_sems, item_sems,
):
    count = steps[0]

    def fetches(number):
        return (
            incoming(ratings, rating_rooms, in_sems, number),
            incoming(sorted_items, item_rooms, item_sems, number),
        )

    def fetch(number):
        @pl.when(number < count)
        def _():
            for copy in fetches(number):
                copy.start()

    for ahead in range(ROOMS - 1):
        fetch(ahead)
    total[...] = jnp.zeros_like(total)

    def step(number, carry):
        room = lax.rem(number, ROOMS)
        fetch(number + ROOMS - 1)
        for copy in fetches(number):
            copy.wait()
        results = []
        for k in range(AT_ONCE):
            user = group_user[number * AT_ONCE + k]
            value = product(False, users[user], rating_rooms[room, k], item_rooms[room, k])
            results.append((user, value))
        for user, value in results:
            total[user] = total[user] + value
        return carry

    lax.fori_loop(0, count, step, 0)
    out[...] = total[...] * (LATER_SCALE / largest(users[...]))


def first_terms(where_to, users, ratings, pieces):
    return pl.pallas_call(
        first_terms_kernel,
        out_shape=[OUT, pltpu.HBM((STEPS, AT_ONCE, GROUP * 128, 128), jnp.bfloat16)],
        in_specs=[SMEM] * 3 + [VMEM] + [ANY] * (1 + len(pieces)),
        out_specs=[VMEM, ANY],
        scratch_shapes=[
            TOTAL,
            pltpu.VMEM((BLOCKS, 128, 128), jnp.bfloat16),
            RATING_ROOMS,
            ITEM_ROOMS,
            pltpu.SemaphoreType.DMA((len(pieces),)),
            ROOM_SEMS,
            ROOM_SEMS,
        ],
        compiler_params=PARAMS,
        cost_estimate=COST,
        name="first_terms",
    )(*where_to, users, in_hbm(ratings), *pieces)


def later_terms(where_to, users, ratings, items):
    return pl.pallas_call(
        later_terms_kernel,
        out_shape=OUT,
        in_specs=[SMEM] * 2 + [VMEM] + [ANY] * 2,
        out_specs=VMEM,
        scratch_shapes=[TOTAL, RATING_ROOMS, ITEM_ROOMS, ROOM_SEMS, ROOM_SEMS],
        compiler_params=PARAMS,
        cost_estimate=COST,
        name="later_terms",
    )(*where_to, users, in_hbm(ratings), in_hbm(items))


def largest(direction):
    size = jnp.max(jnp.abs(direction.astype(jnp.float32)), axis=-1, keepdims=True)
    return jnp.maximum(size, 1e-30)


def to_all(direction, out, unit_out):
    rounded = direction.astype(jnp.bfloat16)
    unit_out[...] = largest(rounded) / LATER_SCALE
    for k in range(out.shape[0]):
        out[k] = rounded


def first_kernel(summed, damping, factors, sent, unit_out, residual_out, squares_out):
    residual = summed[...] / FIRST_SCALE - damping[...] * factors[...]
    residual_out[...] = residual
    squares_out[...] = jnp.sum(residual * residual, axis=1, keepdims=True)
    to_all(residual, sent, unit_out)


def stepped(summed, unit, damping, factors, residual, direction, squares):
    image = summed[...] * unit[...] + damping[...] * direction
    step_size = squares / (jnp.sum(direction * image, axis=1, keepdims=True) + tiny)
    return factors + step_size * direction, residual - step_size * image


def middle_kernel(
    summed, unit, damping, factors, residual, direction, squares,
    sent, unit_out, factors_out, residual_out, direction_out, squares_out,
):
    new_factors, new_residual = stepped(
        summed, unit, damping, factors[...], residual[...], direction[...], squares[...]
    )
    renewed = jnp.sum(new_residual * new_residual, axis=1, keepdims=True)
    new_direction = new_residual + renewed / (squares[...] + tiny) * direction[...]
    factors_out[...] = new_factors
    residual_out[...] = new_residual
    direction_out[...] = new_direction
    squares_out[...] = renewed
    to_all(new_direction, sent, unit_out)


def last_kernel(
    summed, unit, damping, factors, residual, direction, squares, factors_out, residual_out
):
    new_factors, new_residual = stepped(
        summed, unit, damping, factors[...], residual[...], direction[...], squares[...]
    )
    factors_out[...] = new_factors
    residual_out[...] = new_residual


def update(kernel, outs, *args):
    return pl.pallas_call(
        kernel,
        out_shape=outs,
        in_specs=[VMEM] * len(args),
        out_specs=[VMEM] * len(outs),
        compiler_params=pltpu.CompilerParams(vmem_limit_bytes=16 << 20),
        name=kernel.__name__,
    )(*args)


def exchanged(pieces):
    return lax.all_to_all(pieces, RING, 0, 0, tiled=True)


def per_device(user_factors, item_factors, ratings, block_user, block_item, counts):
    own_users, rank = user_factors.shape
    chips = lax.axis_size(RING)
    vector = jax.ShapeDtypeStruct((own_users, rank), jnp.float32)
    scalar = jax.ShapeDtypeStruct((own_users, 1), jnp.float32)
    copies = jax.ShapeDtypeStruct((chips, own_users, rank), jnp.bfloat16)

    own_ratings = ratings[0, 0]
    slot_block, slot_place, group_user, steps = tables(block_user[0, 0], block_item[0, 0])

    def received(sent):
        return exchanged(sent).reshape(LOCAL, 128, rank)

    def summed_up(value):
        parts = exchanged(value.reshape(chips, own_users, rank).astype(jnp.float16))
        return jnp.sum(parts.astype(jnp.float32), axis=0)

    def get_start(line):
        start, unused = lax.optimization_barrier((user_factors, line))
        start = start.astype(jnp.bfloat16)
        return received(jnp.broadcast_to(start[None], copies.shape))

    other_ratings = swapped(own_ratings)
    early = steps * lax.axis_index("core")

    def get_ratings():
        return in_order(slot_block, early, own_ratings, other_ratings)

    damping = jnp.broadcast_to(
        (reg_weight * counts.astype(jnp.float32))[:, None], user_factors.shape
    )
    pieces, users, all_ratings, damping = gathered_items(
        item_factors, damping, get_start, get_ratings
    )
    all_ratings = in_order(
        slot_block, steps - early, own_ratings, other_ratings, all_ratings
    )
    value, items = first_terms(
        (slot_place, group_user, steps), users, all_ratings, pieces
    )
    sent, unit, residual, squares = update(
        first_kernel,
        [copies, scalar, vector, scalar],
        summed_up(value),
        damping,
        user_factors,
    )
    factors, direction = user_factors, residual
    for iteration in range(ITERS):
        summed = summed_up(
            later_terms((group_user, steps), received(sent), all_ratings, items)
        )
        state = (summed, unit, damping, factors, residual, direction, squares)
        if iteration + 1 < ITERS:
            sent, unit, factors, residual, direction, squares = update(
                middle_kernel, [copies, scalar, vector, vector, vector, scalar], *state
            )
        else:
            factors, residual = update(last_kernel, [vector, vector], *state)
    return factors, residual


def solution(mesh):
    fine = Mesh(
        mesh.devices.reshape(4, 4, 4, 2, 2), ("y", "x", "zh", "core", "zl")
    )
    row, col = ("y", "x"), ("zh", "core")
    every = row + col + ("zl",)
    return jax.shard_map(
        per_device,
        mesh=fine,
        in_specs=(
            P(every, None),
            P(row + col, None),
            P(row, col, "zl", None, None),
            P(row, col, "zl"),
            P(row, col, "zl"),
            P(every),
        ),
        out_specs=(P(every, None), P(every, None)),
        check_vma=False,
    )
```

```python
import functools

import jax
import jax.numpy as jnp
from jax import lax
from jax.experimental import pallas as pl
from jax.experimental.pallas import tpu as pltpu
from jax.sharding import Mesh, PartitionSpec as P

ITERS = 2
GROUP = 8
AT_ONCE = 4
BLOCKS = 256
STEP_BLOCKS = GROUP * AT_ONCE
ROOMS = 3
STEPS = BLOCKS // STEP_BLOCKS
LOCAL = 16

FIRST_SCALE = 4.0
LATER_SCALE = 16.0

reg_weight = 0.0004
tiny = 1e-06

RING = ("zh", "zl")
SWAP = [(0, 1), (1, 0)]
VMEM = pl.BlockSpec(memory_space=pltpu.VMEM)
ANY = pl.BlockSpec(memory_space=pl.ANY)
SMEM = pl.BlockSpec(memory_space=pltpu.SMEM)


def in_hbm(array):
    return pltpu.with_memory_space_constraint(array, pltpu.HBM)


def swapped(array):
    return lax.ppermute(array, "core", SWAP)


def turned(array, leg, step):
    pairs = []
    for y in range(4):
        for x in range(4):
            for core in range(2):
                along_x = core == leg
                to_y = y if along_x else (y + step) % 4
                to_x = (x + step) % 4 if along_x else x
                pairs.append(((y * 4 + x) * 2 + core, (to_y * 4 + to_x) * 2 + core))
    return lax.ppermute(array, ("y", "x", "core"), pairs)


def around(near, leg):
    half = near.shape[0] // 2
    behind = turned(near, leg, 1)
    ahead = turned(near, leg, -1)
    far = [turned(behind[:half], leg, 1), turned(ahead[half:], leg, -1)]
    return [near, ahead, *far, behind]


def gathered_items(item_factors, damping, get_start, get_ratings):
    blocks = item_factors.reshape(item_factors.shape[0] // 128, 128, 128)
    near, ahead, *far, behind = around(blocks, 0)
    line = [jnp.concatenate([near, ahead]), jnp.concatenate([*far, behind])]
    behind = [turned(line[0], 1, 1)]
    ahead = [turned(line[1], 1, -1)]
    behind.append(turned(line[1], 1, 1))
    ahead.insert(0, turned(line[0], 1, -1))
    users = get_start(line)
    ratings = get_ratings()
    far = [turned(behind[0], 1, 1), turned(ahead[1], 1, -1)]
    *far, users, ratings, damping = lax.optimization_barrier((*far, users, ratings, damping))
    own = [*line, *ahead, *far, *behind]
    other = [swapped(piece) for piece in own]
    return own + other, users, ratings, damping


def item_places(block_item):
    y, x, core = lax.axis_index("y"), lax.axis_index("x"), lax.axis_index("core")
    dy = ((block_item >> 5) - y) & 3
    dx = ((block_item >> 3) - x) & 3
    first, second = jnp.where(core == 0, dx, dy), jnp.where(core == 0, dy, dx)
    return (second * 4 + first) * 8 + (block_item & 7)


def tables(block_user, block_item):
    own = jnp.stack([block_user, item_places(block_item)])
    other = swapped(own)
    owners = jnp.concatenate([own[0], other[0]])
    places = jnp.concatenate([own[1], other[1] + 128])
    ids = jnp.arange(BLOCKS, dtype=jnp.int32)
    users = jnp.arange(LOCAL, dtype=jnp.int32)
    mine = ((owners >> 2) & 1) == lax.axis_index("core")
    local = jnp.where(mine, ((owners >> 3) << 2) | (owners & 3), LOCAL)
    before = (local[None, :] == local[:, None]) & (ids[None, :] < ids[:, None])
    position = jnp.sum(before.astype(jnp.int32), axis=1)
    members = jnp.sum((local[None, :] == users[:, None]).astype(jnp.int32), axis=1)
    groups = (members + GROUP - 1) // GROUP
    start = jnp.sum(
        jnp.where(users[None, :] < local[:, None], groups[None, :], 0), axis=1
    )
    ends = jnp.sum(
        jnp.where(users[None, :] <= users[:, None], groups[None, :], 0), axis=1
    )
    slot = jnp.where(mine, start * GROUP + position, BLOCKS)
    here = mine[None, :] & (slot[None, :] == ids[:, None])
    slot_block = BLOCKS + jnp.sum(jnp.where(here, ids[None, :] - BLOCKS, 0), axis=1)
    slot_place = jnp.sum(jnp.where(here, places[None, :], 0), axis=1)
    group_ids = jnp.arange(BLOCKS // GROUP, dtype=jnp.int32)
    group_user = jnp.sum((ends[None, :] <= group_ids[:, None]).astype(jnp.int32), axis=1)
    group_user = jnp.minimum(group_user, LOCAL - 1)
    steps = (ends[LOCAL - 1 :] + AT_ONCE - 1) // AT_ONCE
    return slot_block, slot_place, group_user, steps


OUT = jax.ShapeDtypeStruct((LOCAL, 128, 128), jnp.float32)
TOTAL = pltpu.VMEM((LOCAL, 128, 128), jnp.float32)
RATING_ROOMS = pltpu.VMEM((ROOMS, AT_ONCE, 128, GROUP * 128), jnp.bfloat16)
ITEM_ROOMS = pltpu.VMEM((ROOMS, AT_ONCE, GROUP * 128, 128), jnp.bfloat16)
ROOM_SEMS = pltpu.SemaphoreType.DMA((ROOMS,))
PARAMS = pltpu.CompilerParams(vmem_limit_bytes=24 << 20)
COST = pl.CostEstimate(flops=1 << 30, bytes_accessed=12 << 20, transcendentals=0)


def sort_kernel(slot_block, steps, own, other, *refs):
    out, whole, rooms, sems, out_sems = refs[-5:]
    count = steps[0]
    half = BLOCKS // 2
    copies = [
        pltpu.make_async_copy(own, whole.at[pl.ds(0, half)], sems.at[0]),
        pltpu.make_async_copy(other, whole.at[pl.ds(half, half)], sems.at[1]),
    ]

    @pl.when(count > 0)
    def _():
        for copy in copies:
            copy.start()
        for copy in copies:
            copy.wait()

    def outgoing(number):
        room = lax.rem(number, ROOMS)
        return pltpu.make_async_copy(rooms.at[room], out.at[number], out_sems.at[room])

    def step(number, carry):
        room = lax.rem(number, ROOMS)

        @pl.when(number >= ROOMS)
        def _():
            outgoing(number - ROOMS).wait()

        for k in range(STEP_BLOCKS):
            block = slot_block[number * STEP_BLOCKS + k]
            values = whole[jnp.minimum(block, BLOCKS - 1)]
            lane = (k % GROUP) * 128
            rooms[room, k // GROUP, :, lane : lane + 128] = jnp.where(
                block < BLOCKS, values, jnp.bfloat16(0)
            )
        outgoing(number).start()
        return carry

    lax.fori_loop(0, count, step, 0)
    for back in range(1, ROOMS + 1):

        @pl.when(count >= back)
        def _():
            outgoing(jnp.maximum(count - back, 0)).wait()


def in_order(slot_block, steps, own, other, *earlier):
    return pl.pallas_call(
        sort_kernel,
        out_shape=pltpu.HBM((STEPS, AT_ONCE, 128, GROUP * 128), jnp.bfloat16),
        in_specs=[SMEM] * 2 + [ANY] * (2 + len(earlier)),
        out_specs=ANY,
        input_output_aliases={4: 0} if earlier else {},
        scratch_shapes=[
            pltpu.VMEM((BLOCKS, 128, 128), jnp.bfloat16),
            RATING_ROOMS,
            pltpu.SemaphoreType.DMA((2,)),
            ROOM_SEMS,
        ],
        compiler_params=PARAMS,
        cost_estimate=pl.CostEstimate(flops=0, bytes_accessed=20 << 20, transcendentals=0),
        name="in_order",
    )(slot_block, steps, in_hbm(own), in_hbm(other), *[in_hbm(array) for array in earlier])


def product(with_ratings, user_rows, rating, item_rows):
    predicted = lax.dot_general(
        user_rows, item_rows, (((1,), (1,)), ((), ())), preferred_element_type=jnp.float32
    )
    if with_ratings:
        weights = jnp.where(
            rating != 0, rating.astype(jnp.float32) - predicted, 0.0
        ).astype(jnp.bfloat16)
    else:
        weights = jnp.where(rating != 0, predicted.astype(jnp.bfloat16), jnp.bfloat16(0))
    return jnp.dot(weights, item_rows, preferred_element_type=jnp.float32)


def incoming(source, rooms, sems, number):
    room = lax.rem(number, ROOMS)
    return pltpu.make_async_copy(
        source.at[jnp.minimum(number, STEPS - 1)], rooms.at[room], sems.at[room]
    )


def first_terms_kernel(slot_place, group_user, steps, users, ratings, *refs):
    *pieces, out, sorted_items, total, whole, rating_rooms, item_rooms, sems, in_sems, out_sems = refs
    count = steps[0]
    copies, place = [], 0
    for number, piece in enumerate(pieces):
        extent = piece.shape[0]
        copies.append(
            pltpu.make_async_copy(piece, whole.at[pl.ds(place, extent)], sems.at[number])
        )
        place += extent
    for copy in copies:
        copy.start()
    def fetch(number):
        @pl.when(number < count)
        def _():
            incoming(ratings, rating_rooms, in_sems, number).start()

    for ahead in range(ROOMS - 1):
        fetch(ahead)
    total[...] = jnp.zeros_like(total)
    for copy in copies:
        copy.wait()

    def outgoing(number):
        room = lax.rem(number, ROOMS)
        return pltpu.make_async_copy(
            item_rooms.at[room], sorted_items.at[number], out_sems.at[room]
        )

    def step(number, carry):
        room = lax.rem(number, ROOMS)

        @pl.when(number >= ROOMS)
        def _():
            outgoing(number - ROOMS).wait()

        fetch(number + ROOMS - 1)
        incoming(ratings, rating_rooms, in_sems, number).wait()
        results = []
        for k in range(AT_ONCE):
            first = (number * AT_ONCE + k) * GROUP
            item_rows = jnp.concatenate(
                [whole[slot_place[first + i]] for i in range(GROUP)], axis=0
            )
            item_rooms[room, k] = item_rows
            user = group_user[number * AT_ONCE + k]
            start = users[user].astype(jnp.bfloat16)
            results.append((user, product(True, start, rating_rooms[room, k], item_rows)))
        for user, value in results:
            total[user] = total[user] + value
        outgoing(number).start()
        return carry

    lax.fori_loop(0, count, step, 0)
    out[...] = total[...] * FIRST_SCALE
    for back in range(1, ROOMS + 1):

        @pl.when(count >= back)
        def _():
            outgoing(jnp.maximum(count - back, 0)).wait()


def later_terms_kernel(
    group_user, steps, users, ratings, sorted_items,
    out, total, rating_rooms, item_rooms, in_sems, item_sems,
):
    count = steps[0]

    def fetches(number):
        return (
            incoming(ratings, rating_rooms, in_sems, number),
            incoming(sorted_items, item_rooms, item_sems, number),
        )

    def fetch(number):
        @pl.when(number < count)
        def _():
            for copy in fetches(number):
                copy.start()

    for ahead in range(ROOMS - 1):
        fetch(ahead)
    total[...] = jnp.zeros_like(total)

    def step(number, carry):
        room = lax.rem(number, ROOMS)
        fetch(number + ROOMS - 1)
        for copy in fetches(number):
            copy.wait()
        results = []
        for k in range(AT_ONCE):
            user = group_user[number * AT_ONCE + k]
            value = product(False, users[user], rating_rooms[room, k], item_rooms[room, k])
            results.append((user, value))
        for user, value in results:
            total[user] = total[user] + value
        return carry

    lax.fori_loop(0, count, step, 0)
    out[...] = total[...] * (LATER_SCALE / largest(users[...]))


def first_terms(where_to, users, ratings, pieces):
    return pl.pallas_call(
        first_terms_kernel,
        out_shape=[OUT, pltpu.HBM((STEPS, AT_ONCE, GROUP * 128, 128), jnp.bfloat16)],
        in_specs=[SMEM] * 3 + [VMEM] + [ANY] * (1 + len(pieces)),
        out_specs=[VMEM, ANY],
        scratch_shapes=[
            TOTAL,
            pltpu.VMEM((BLOCKS, 128, 128), jnp.bfloat16),
            RATING_ROOMS,
            ITEM_ROOMS,
            pltpu.SemaphoreType.DMA((len(pieces),)),
            ROOM_SEMS,
            ROOM_SEMS,
        ],
        compiler_params=PARAMS,
        cost_estimate=COST,
        name="first_terms",
    )(*where_to, users, in_hbm(ratings), *pieces)


def later_terms(where_to, users, ratings, items):
    return pl.pallas_call(
        later_terms_kernel,
        out_shape=OUT,
        in_specs=[SMEM] * 2 + [VMEM] + [ANY] * 2,
        out_specs=VMEM,
        scratch_shapes=[TOTAL, RATING_ROOMS, ITEM_ROOMS, ROOM_SEMS, ROOM_SEMS],
        compiler_params=PARAMS,
        cost_estimate=COST,
        name="later_terms",
    )(*where_to, users, in_hbm(ratings), in_hbm(items))


def largest(direction):
    size = jnp.max(jnp.abs(direction.astype(jnp.float32)), axis=-1, keepdims=True)
    return jnp.maximum(size, 1e-30)


def to_all(direction, out, unit_out):
    rounded = direction.astype(jnp.bfloat16)
    unit_out[...] = largest(rounded) / LATER_SCALE
    for k in range(out.shape[0]):
        out[k] = rounded


def first_kernel(summed, damping, factors, sent, unit_out, residual_out, squares_out):
    residual = summed[...] / FIRST_SCALE - damping[...] * factors[...]
    residual_out[...] = residual
    squares_out[...] = jnp.sum(residual * residual, axis=1, keepdims=True)
    to_all(residual, sent, unit_out)


def stepped(summed, unit, damping, factors, residual, direction, squares):
    image = summed[...] * unit[...] + damping[...] * direction
    step_size = squares / (jnp.sum(direction * image, axis=1, keepdims=True) + tiny)
    return factors + step_size * direction, residual - step_size * image


def middle_kernel(
    summed, unit, damping, factors, residual, direction, squares,
    sent, unit_out, factors_out, residual_out, direction_out, squares_out,
):
    new_factors, new_residual = stepped(
        summed, unit, damping, factors[...], residual[...], direction[...], squares[...]
    )
    renewed = jnp.sum(new_residual * new_residual, axis=1, keepdims=True)
    new_direction = new_residual + renewed / (squares[...] + tiny) * direction[...]
    factors_out[...] = new_factors
    residual_out[...] = new_residual
    direction_out[...] = new_direction
    squares_out[...] = renewed
    to_all(new_direction, sent, unit_out)


def last_kernel(
    summed, unit, damping, factors, residual, direction, squares, factors_out, residual_out
):
    new_factors, new_residual = stepped(
        summed, unit, damping, factors[...], residual[...], direction[...], squares[...]
    )
    factors_out[...] = new_factors
    residual_out[...] = new_residual


def update(kernel, outs, *args):
    return pl.pallas_call(
        kernel,
        out_shape=outs,
        in_specs=[VMEM] * len(args),
        out_specs=[VMEM] * len(outs),
        compiler_params=pltpu.CompilerParams(vmem_limit_bytes=16 << 20),
        name=kernel.__name__,
    )(*args)


def exchanged(pieces):
    return lax.all_to_all(pieces, RING, 0, 0, tiled=True)


def per_device(user_factors, item_factors, ratings, block_user, block_item, counts):
    own_users, rank = user_factors.shape
    chips = lax.axis_size(RING)
    vector = jax.ShapeDtypeStruct((own_users, rank), jnp.float32)
    scalar = jax.ShapeDtypeStruct((own_users, 1), jnp.float32)
    copies = jax.ShapeDtypeStruct((chips, own_users, rank), jnp.bfloat16)

    own_ratings = ratings[0, 0]
    slot_block, slot_place, group_user, steps = tables(block_user[0, 0], block_item[0, 0])

    def received(sent):
        return exchanged(sent).reshape(LOCAL, 128, rank)

    def summed_up(value):
        parts = exchanged(value.reshape(chips, own_users, rank).astype(jnp.float16))
        return jnp.sum(parts.astype(jnp.float32), axis=0)

    def get_start(line):
        start, unused = lax.optimization_barrier((user_factors, line))
        start = start.astype(jnp.bfloat16)
        return received(jnp.broadcast_to(start[None], copies.shape))

    other_ratings = swapped(own_ratings)
    early = steps * lax.axis_index("core")

    def get_ratings():
        return in_order(slot_block, early, own_ratings, other_ratings)

    damping = jnp.broadcast_to(
        (reg_weight * counts.astype(jnp.float32))[:, None], user_factors.shape
    )
    pieces, users, all_ratings, damping = gathered_items(
        item_factors, damping, get_start, get_ratings
    )
    all_ratings = in_order(
        slot_block, steps - early, own_ratings, other_ratings, all_ratings
    )
    value, items = first_terms(
        (slot_place, group_user, steps), users, all_ratings, pieces
    )
    sent, unit, residual, squares = update(
        first_kernel,
        [copies, scalar, vector, scalar],
        summed_up(value),
        damping,
        user_factors,
    )
    factors, direction = user_factors, residual
    for iteration in range(ITERS):
        summed = summed_up(
            later_terms((group_user, steps), received(sent), all_ratings, items)
        )
        state = (summed, unit, damping, factors, residual, direction, squares)
        if iteration + 1 < ITERS:
            sent, unit, factors, residual, direction, squares = update(
                middle_kernel, [copies, scalar, vector, vector, vector, scalar], *state
            )
        else:
            factors, residual = update(last_kernel, [vector, vector], *state)
    return factors, residual


def solution(mesh):
    fine = Mesh(
        mesh.devices.reshape(4, 4, 4, 2, 2), ("y", "x", "zh", "core", "zl")
    )
    row, col = ("y", "x"), ("zh", "core")
    every = row + col + ("zl",)
    return jax.shard_map(
        per_device,
        mesh=fine,
        in_specs=(
            P(every, None),
            P(row + col, None),
            P(row, col, "zl", None, None),
            P(row, col, "zl"),
            P(row, col, "zl"),
            P(every),
        ),
        out_specs=(P(every, None), P(every, None)),
        check_vma=False,
    )
```

```python
import functools

import jax
import jax.numpy as jnp
from jax import lax
from jax.experimental import pallas as pl
from jax.experimental.pallas import tpu as pltpu
from jax.sharding import Mesh, PartitionSpec as P

ITERS = 2
GROUP = 8
AT_ONCE = 4
BLOCKS = 256
STEP_BLOCKS = GROUP * AT_ONCE
ROOMS = 3
STEPS = BLOCKS // STEP_BLOCKS
LOCAL = 16

FIRST_SCALE = 4.0
LATER_SCALE = 16.0

reg_weight = 0.0004
tiny = 1e-06

RING = ("zh", "zl")
SWAP = [(0, 1), (1, 0)]
VMEM = pl.BlockSpec(memory_space=pltpu.VMEM)
ANY = pl.BlockSpec(memory_space=pl.ANY)
SMEM = pl.BlockSpec(memory_space=pltpu.SMEM)


def in_hbm(array):
    return pltpu.with_memory_space_constraint(array, pltpu.HBM)


def swapped(array):
    return lax.ppermute(array, "core", SWAP)


def turned(array, leg, step):
    pairs = []
    for y in range(4):
        for x in range(4):
            for core in range(2):
                along_x = core == leg
                to_y = y if along_x else (y + step) % 4
                to_x = (x + step) % 4 if along_x else x
                pairs.append(((y * 4 + x) * 2 + core, (to_y * 4 + to_x) * 2 + core))
    return lax.ppermute(array, ("y", "x", "core"), pairs)


def around(near, leg):
    half = near.shape[0] // 2
    behind = turned(near, leg, 1)
    ahead = turned(near, leg, -1)
    far = [turned(behind[:half], leg, 1), turned(ahead[half:], leg, -1)]
    return [near, ahead, *far, behind]


def gathered_items(item_factors, damping, get_start, get_ratings):
    blocks = item_factors.reshape(item_factors.shape[0] // 128, 128, 128)
    near, ahead, *far, behind = around(blocks, 0)
    line = [jnp.concatenate([near, ahead]), jnp.concatenate([*far, behind])]
    behind = [turned(line[0], 1, 1)]
    ahead = [turned(line[1], 1, -1)]
    behind.append(turned(line[1], 1, 1))
    ahead.insert(0, turned(line[0], 1, -1))
    users = get_start(line)
    ratings = get_ratings()
    far = [turned(behind[0], 1, 1), turned(ahead[1], 1, -1)]
    *far, users, ratings, damping = lax.optimization_barrier((*far, users, ratings, damping))
    own = [*line, *ahead, *far, *behind]
    other = [swapped(piece) for piece in own]
    return own + other, users, ratings, damping


def item_places(block_item):
    y, x, core = lax.axis_index("y"), lax.axis_index("x"), lax.axis_index("core")
    dy = ((block_item >> 5) - y) & 3
    dx = ((block_item >> 3) - x) & 3
    first, second = jnp.where(core == 0, dx, dy), jnp.where(core == 0, dy, dx)
    return (second * 4 + first) * 8 + (block_item & 7)


def tables(block_user, block_item):
    own = jnp.stack([block_user, item_places(block_item)])
    other = swapped(own)
    owners = jnp.concatenate([own[0], other[0]])
    places = jnp.concatenate([own[1], other[1] + 128])
    ids = jnp.arange(BLOCKS, dtype=jnp.int32)
    users = jnp.arange(LOCAL, dtype=jnp.int32)
    mine = ((owners >> 2) & 1) == lax.axis_index("core")
    local = jnp.where(mine, ((owners >> 3) << 2) | (owners & 3), LOCAL)
    before = (local[None, :] == local[:, None]) & (ids[None, :] < ids[:, None])
    position = jnp.sum(before.astype(jnp.int32), axis=1)
    members = jnp.sum((local[None, :] == users[:, None]).astype(jnp.int32), axis=1)
    groups = (members + GROUP - 1) // GROUP
    start = jnp.sum(
        jnp.where(users[None, :] < local[:, None], groups[None, :], 0), axis=1
    )
    ends = jnp.sum(
        jnp.where(users[None, :] <= users[:, None], groups[None, :], 0), axis=1
    )
    slot = jnp.where(mine, start * GROUP + position, BLOCKS)
    here = mine[None, :] & (slot[None, :] == ids[:, None])
    slot_block = BLOCKS + jnp.sum(jnp.where(here, ids[None, :] - BLOCKS, 0), axis=1)
    slot_place = jnp.sum(jnp.where(here, places[None, :], 0), axis=1)
    group_ids = jnp.arange(BLOCKS // GROUP, dtype=jnp.int32)
    group_user = jnp.sum((ends[None, :] <= group_ids[:, None]).astype(jnp.int32), axis=1)
    group_user = jnp.minimum(group_user, LOCAL - 1)
    steps = (ends[LOCAL - 1 :] + AT_ONCE - 1) // AT_ONCE
    return slot_block, slot_place, group_user, steps


OUT = jax.ShapeDtypeStruct((LOCAL, 128, 128), jnp.float32)
TOTAL = pltpu.VMEM((LOCAL, 128, 128), jnp.float32)
RATING_ROOMS = pltpu.VMEM((ROOMS, AT_ONCE, 128, GROUP * 128), jnp.bfloat16)
ITEM_ROOMS = pltpu.VMEM((ROOMS, AT_ONCE, GROUP * 128, 128), jnp.bfloat16)
ROOM_SEMS = pltpu.SemaphoreType.DMA((ROOMS,))
PARAMS = pltpu.CompilerParams(vmem_limit_bytes=24 << 20)
COST = pl.CostEstimate(flops=1 << 30, bytes_accessed=12 << 20, transcendentals=0)


def sort_kernel(slot_block, steps, own, other, *refs):
    out, whole, rooms, sems, out_sems = refs[-5:]
    count = steps[0]
    half = BLOCKS // 2
    copies = [
        pltpu.make_async_copy(own, whole.at[pl.ds(0, half)], sems.at[0]),
        pltpu.make_async_copy(other, whole.at[pl.ds(half, half)], sems.at[1]),
    ]

    @pl.when(count > 0)
    def _():
        for copy in copies:
            copy.start()
        for copy in copies:
            copy.wait()

    def outgoing(number):
        room = lax.rem(number, ROOMS)
        return pltpu.make_async_copy(rooms.at[room], out.at[number], out_sems.at[room])

    def step(number, carry):
        room = lax.rem(number, ROOMS)

        @pl.when(number >= ROOMS)
        def _():
            outgoing(number - ROOMS).wait()

        for k in range(STEP_BLOCKS):
            block = slot_block[number * STEP_BLOCKS + k]
            values = whole[jnp.minimum(block, BLOCKS - 1)]
            lane = (k % GROUP) * 128
            rooms[room, k // GROUP, :, lane : lane + 128] = jnp.where(
                block < BLOCKS, values, jnp.bfloat16(0)
            )
        outgoing(number).start()
        return carry

    lax.fori_loop(0, count, step, 0)
    for back in range(1, ROOMS + 1):

        @pl.when(count >= back)
        def _():
            outgoing(jnp.maximum(count - back, 0)).wait()


def in_order(slot_block, steps, own, other, *earlier):
    return pl.pallas_call(
        sort_kernel,
        out_shape=pltpu.HBM((STEPS, AT_ONCE, 128, GROUP * 128), jnp.bfloat16),
        in_specs=[SMEM] * 2 + [ANY] * (2 + len(earlier)),
        out_specs=ANY,
        input_output_aliases={4: 0} if earlier else {},
        scratch_shapes=[
            pltpu.VMEM((BLOCKS, 128, 128), jnp.bfloat16),
            RATING_ROOMS,
            pltpu.SemaphoreType.DMA((2,)),
            ROOM_SEMS,
        ],
        compiler_params=PARAMS,
        cost_estimate=pl.CostEstimate(flops=0, bytes_accessed=20 << 20, transcendentals=0),
        name="in_order",
    )(slot_block, steps, in_hbm(own), in_hbm(other), *[in_hbm(array) for array in earlier])


def product(with_ratings, user_rows, rating, item_rows):
    predicted = lax.dot_general(
        user_rows, item_rows, (((1,), (1,)), ((), ())), preferred_element_type=jnp.float32
    )
    if with_ratings:
        weights = jnp.where(
            rating != 0, rating.astype(jnp.float32) - predicted, 0.0
        ).astype(jnp.bfloat16)
    else:
        weights = jnp.where(rating != 0, predicted.astype(jnp.bfloat16), jnp.bfloat16(0))
    return jnp.dot(weights, item_rows, preferred_element_type=jnp.float32)


def incoming(source, rooms, sems, number):
    room = lax.rem(number, ROOMS)
    return pltpu.make_async_copy(
        source.at[jnp.minimum(number, STEPS - 1)], rooms.at[room], sems.at[room]
    )


def first_terms_kernel(slot_place, group_user, steps, users, ratings, *refs):
    *pieces, out, sorted_items, total, whole, rating_rooms, item_rooms, sems, in_sems, out_sems = refs
    count = steps[0]
    copies, place = [], 0
    for number, piece in enumerate(pieces):
        extent = piece.shape[0]
        copies.append(
            pltpu.make_async_copy(piece, whole.at[pl.ds(place, extent)], sems.at[number])
        )
        place += extent
    for copy in copies:
        copy.start()
    def fetch(number):
        @pl.when(number < count)
        def _():
            incoming(ratings, rating_rooms, in_sems, number).start()

    for ahead in range(ROOMS - 1):
        fetch(ahead)
    total[...] = jnp.zeros_like(total)
    for copy in copies:
        copy.wait()

    def outgoing(number):
        room = lax.rem(number, ROOMS)
        return pltpu.make_async_copy(
            item_rooms.at[room], sorted_items.at[number], out_sems.at[room]
        )

    def step(number, carry):
        room = lax.rem(number, ROOMS)

        @pl.when(number >= ROOMS)
        def _():
            outgoing(number - ROOMS).wait()

        fetch(number + ROOMS - 1)
        incoming(ratings, rating_rooms, in_sems, number).wait()
        results = []
        for k in range(AT_ONCE):
            first = (number * AT_ONCE + k) * GROUP
            item_rows = jnp.concatenate(
                [whole[slot_place[first + i]] for i in range(GROUP)], axis=0
            )
            item_rooms[room, k] = item_rows
            user = group_user[number * AT_ONCE + k]
            start = users[user].astype(jnp.bfloat16)
            results.append((user, product(True, start, rating_rooms[room, k], item_rows)))
        for user, value in results:
            total[user] = total[user] + value
        outgoing(number).start()
        return carry

    lax.fori_loop(0, count, step, 0)
    out[...] = total[...] * FIRST_SCALE
    for back in range(1, ROOMS + 1):

        @pl.when(count >= back)
        def _():
            outgoing(jnp.maximum(count - back, 0)).wait()


def later_terms_kernel(
    group_user, steps, users, ratings, sorted_items,
    out, total, rating_rooms, item_rooms, in_sems, item_sems,
):
    count = steps[0]

    def fetches(number):
        return (
            incoming(ratings, rating_rooms, in_sems, number),
            incoming(sorted_items, item_rooms, item_sems, number),
        )

    def fetch(number):
        @pl.when(number < count)
        def _():
            for copy in fetches(number):
                copy.start()

    for ahead in range(ROOMS - 1):
        fetch(ahead)
    total[...] = jnp.zeros_like(total)

    def step(number, carry):
        room = lax.rem(number, ROOMS)
        fetch(number + ROOMS - 1)
        for copy in fetches(number):
            copy.wait()
        results = []
        for k in range(AT_ONCE):
            user = group_user[number * AT_ONCE + k]
            value = product(False, users[user], rating_rooms[room, k], item_rooms[room, k])
            results.append((user, value))
        for user, value in results:
            total[user] = total[user] + value
        return carry

    lax.fori_loop(0, count, step, 0)
    out[...] = total[...] * (LATER_SCALE / largest(users[...]))


def first_terms(where_to, users, ratings, pieces):
    return pl.pallas_call(
        first_terms_kernel,
        out_shape=[OUT, pltpu.HBM((STEPS, AT_ONCE, GROUP * 128, 128), jnp.bfloat16)],
        in_specs=[SMEM] * 3 + [VMEM] + [ANY] * (1 + len(pieces)),
        out_specs=[VMEM, ANY],
        scratch_shapes=[
            TOTAL,
            pltpu.VMEM((BLOCKS, 128, 128), jnp.bfloat16),
            RATING_ROOMS,
            ITEM_ROOMS,
            pltpu.SemaphoreType.DMA((len(pieces),)),
            ROOM_SEMS,
            ROOM_SEMS,
        ],
        compiler_params=PARAMS,
        cost_estimate=COST,
        name="first_terms",
    )(*where_to, users, in_hbm(ratings), *pieces)


def later_terms(where_to, users, ratings, items):
    return pl.pallas_call(
        later_terms_kernel,
        out_shape=OUT,
        in_specs=[SMEM] * 2 + [VMEM] + [ANY] * 2,
        out_specs=VMEM,
        scratch_shapes=[TOTAL, RATING_ROOMS, ITEM_ROOMS, ROOM_SEMS, ROOM_SEMS],
        compiler_params=PARAMS,
        cost_estimate=COST,
        name="later_terms",
    )(*where_to, users, in_hbm(ratings), in_hbm(items))


def largest(direction):
    size = jnp.max(jnp.abs(direction.astype(jnp.float32)), axis=-1, keepdims=True)
    return jnp.maximum(size, 1e-30)


def to_all(direction, out, unit_out):
    rounded = direction.astype(jnp.bfloat16)
    unit_out[...] = largest(rounded) / LATER_SCALE
    for k in range(out.shape[0]):
        out[k] = rounded


def first_kernel(summed, damping, factors, sent, unit_out, residual_out, squares_out):
    residual = summed[...] / FIRST_SCALE - damping[...] * factors[...]
    residual_out[...] = residual
    squares_out[...] = jnp.sum(residual * residual, axis=1, keepdims=True)
    to_all(residual, sent, unit_out)


def stepped(summed, unit, damping, factors, residual, direction, squares):
    image = summed[...] * unit[...] + damping[...] * direction
    step_size = squares / (jnp.sum(direction * image, axis=1, keepdims=True) + tiny)
    return factors + step_size * direction, residual - step_size * image


def middle_kernel(
    summed, unit, damping, factors, residual, direction, squares,
    sent, unit_out, factors_out, residual_out, direction_out, squares_out,
):
    new_factors, new_residual = stepped(
        summed, unit, damping, factors[...], residual[...], direction[...], squares[...]
    )
    renewed = jnp.sum(new_residual * new_residual, axis=1, keepdims=True)
    new_direction = new_residual + renewed / (squares[...] + tiny) * direction[...]
    factors_out[...] = new_factors
    residual_out[...] = new_residual
    direction_out[...] = new_direction
    squares_out[...] = renewed
    to_all(new_direction, sent, unit_out)


def last_kernel(
    summed, unit, damping, factors, residual, direction, squares, factors_out, residual_out
):
    new_factors, new_residual = stepped(
        summed, unit, damping, factors[...], residual[...], direction[...], squares[...]
    )
    factors_out[...] = new_factors
    residual_out[...] = new_residual


def update(kernel, outs, *args):
    return pl.pallas_call(
        kernel,
        out_shape=outs,
        in_specs=[VMEM] * len(args),
        out_specs=[VMEM] * len(outs),
        compiler_params=pltpu.CompilerParams(vmem_limit_bytes=16 << 20),
        name=kernel.__name__,
    )(*args)


def exchanged(pieces):
    return lax.all_to_all(pieces, RING, 0, 0, tiled=True)


def per_device(user_factors, item_factors, ratings, block_user, block_item, counts):
    own_users, rank = user_factors.shape
    chips = lax.axis_size(RING)
    vector = jax.ShapeDtypeStruct((own_users, rank), jnp.float32)
    scalar = jax.ShapeDtypeStruct((own_users, 1), jnp.float32)
    copies = jax.ShapeDtypeStruct((chips, own_users, rank), jnp.bfloat16)

    own_ratings = ratings[0, 0]
    slot_block, slot_place, group_user, steps = tables(block_user[0, 0], block_item[0, 0])

    def received(sent):
        return exchanged(sent).reshape(LOCAL, 128, rank)

    def summed_up(value):
        parts = exchanged(value.reshape(chips, own_users, rank).astype(jnp.float16))
        return jnp.sum(parts.astype(jnp.float32), axis=0)

    def get_start(line):
        start = user_factors.astype(jnp.bfloat16)
        start = jnp.broadcast_to(start[None], copies.shape)
        start, unused = lax.optimization_barrier((start, line))
        return received(start)

    other_ratings = swapped(own_ratings)
    early = steps * lax.axis_index("core")

    def get_ratings():
        return in_order(slot_block, early, own_ratings, other_ratings)

    damping = jnp.broadcast_to(
        (reg_weight * counts.astype(jnp.float32))[:, None], user_factors.shape
    )
    pieces, users, all_ratings, damping = gathered_items(
        item_factors, damping, get_start, get_ratings
    )
    all_ratings = in_order(
        slot_block, steps - early, own_ratings, other_ratings, all_ratings
    )
    value, items = first_terms(
        (slot_place, group_user, steps), users, all_ratings, pieces
    )
    sent, unit, residual, squares = update(
        first_kernel,
        [copies, scalar, vector, scalar],
        summed_up(value),
        damping,
        user_factors,
    )
    factors, direction = user_factors, residual
    for iteration in range(ITERS):
        summed = summed_up(
            later_terms((group_user, steps), received(sent), all_ratings, items)
        )
        state = (summed, unit, damping, factors, residual, direction, squares)
        if iteration + 1 < ITERS:
            sent, unit, factors, residual, direction, squares = update(
                middle_kernel, [copies, scalar, vector, vector, vector, scalar], *state
            )
        else:
            factors, residual = update(last_kernel, [vector, vector], *state)
    return factors, residual


def solution(mesh):
    fine = Mesh(
        mesh.devices.reshape(4, 4, 4, 2, 2), ("y", "x", "zh", "core", "zl")
    )
    row, col = ("y", "x"), ("zh", "core")
    every = row + col + ("zl",)
    return jax.shard_map(
        per_device,
        mesh=fine,
        in_specs=(
            P(every, None),
            P(row + col, None),
            P(row, col, "zl", None, None),
            P(row, col, "zl"),
            P(row, col, "zl"),
            P(every),
        ),
        out_specs=(P(every, None), P(every, None)),
        check_vma=False,
    )
```
